32 devices in a mesh: groups: 2 (over y), seq: 4 (over z), res: 4 (over x, core).
Axes of the slice: x: 2, y: 2, z: 4, core: 2. Of those that a mesh axis runs over, the one named last changes fastest.
Arguments:
- alignment: float32 [256, 64, 64], P(('groups', 'seq'), 'res'), parts along dimension 0, may hold values from -100 to 100
- seq_mask: int32 [256, 64], P(('groups', 'seq'), 'res'), parts along dimension 0, may hold values from 0 to 1, as said below
- pair_rep: float32 [128, 64, 128], P(('groups', 'res'), 'seq'), parts along dimension 0, may hold values from -6 to 6
- chain_index: int32 [128], P('groups'), parts along dimension 0, may hold values from 0 to 3, never falling along the last dimension, each value on 1 to 32 neighbouring positions
- rel_table: float32 [66, 128], replicated, may hold values from -3 to 3
- w_factors: bfloat16 [64, 64], replicated, may hold values from -0.75 to 0.75
- w_outer: float32 [1024, 128], replicated, may hold values from -0.1875 to 0.1875
- w_bias: float32 [128, 8], replicated, may hold values from -1.5 to 1.5
- w_attention: bfloat16 [64, 256], replicated, may hold values from -30 to 30
- w_output: bfloat16 [64, 64], replicated, may hold values from -0.75 to 0.75
Outputs:
- pair_next: float32 [128, 64, 128], P(('groups', 'res'), 'seq'), parts along dimension 0
- alignment_next: float32 [256, 64, 64], P(('groups', 'seq'), 'res'), parts along dimension 0
The draws below stay inside these ranges and needn't reach their ends.
There are 2 independent parts, one for each index of `groups`. The reference program is written for one: setup_inputs(seed, part) draws one part's arguments, and reference() takes and returns one part's arrays. A program takes and returns all parts, laid end to end along the dimension named above; an argument that names none is the same for every part. Nothing has to cross between parts.
Inputs may be any that keep to these rules, and one draw needn't show every extreme that they name: `seq_mask`: some residues at the end, at least the last one, are padding: 0 in every sequence. `chain_index`: chain index of a residue, never falling along the residues.
All inputs are finite; a program needn't handle non-finite values.
Results may differ from the reference program's by a relative error of at most 0.0015.
Values may be sent and summed in bfloat16 or wider, within the bound.
A program may use at most 64 MiB of HBM per device.

```python
import math
import jax
import jax.numpy as jnp
import numpy as np
from jax import lax

C = 64
CO = 32
CZ = 128
HEADS = 8
HD = 8
RELMAX = 32
SEQ_DEV = 32
RES_DEV = 16
S = 128
R = 64
BINS = 66


def draw_alignment(key, part):
    profile = jnp.clip(jax.random.normal(jax.random.fold_in(key, 1), (R, C), jnp.float32), -4.0, 4.0)
    noise = jnp.clip(jax.random.normal(jax.random.fold_in(key, 2), (S, R, C), jnp.float32), -5.0, 5.0)
    return 0.8 * profile[None] + noise


def draw_seq_mask(key, part):
    padding = jax.random.randint(jax.random.fold_in(key, 1), (), 1, R // 8 + 1)
    valid = jnp.arange(R, dtype=jnp.int32) < R - padding
    levels = jax.random.randint(jax.random.fold_in(key, 2), (S, R), 0, 1000)
    limits = 300 + 650 * jnp.arange(S, dtype=jnp.int32) // S
    return ((levels < limits[:, None]) & valid[None, :]).astype(jnp.int32)


def draw_w_attention(key, part):
    base = jnp.clip(jax.random.normal(jax.random.fold_in(key, 1), (C, 4, HEADS, HD), jnp.float32), -4.0, 4.0) * C ** (-0.5)
    return base.reshape(C, 4 * HEADS * HD).astype(jnp.bfloat16)


def block_scale(key, shape, shards, smallest, top_value):
    level, own = 1.0, jax.random.fold_in(key, 6)
    for dim, parts in shards:
        heights = jnp.exp(jax.random.uniform(jax.random.fold_in(own, dim), (parts,), jnp.float32, smallest / len(shards), top_value / len(shards)))
        level = level * jnp.repeat(heights, shape[dim] // parts).reshape([-1 if axis == dim else 1 for axis in range(len(shape))])
    return level


def length_profile(count, total, most, lean):
    loads = [(1 << 20) // math.isqrt(standing ** lean) + 1 for standing in range(2, count + 1)]
    surplus, given = total - most - (count - 1), [1] * (count - 1)
    while surplus > 0:
        movable = [i for i in range(count - 1) if given[i] < most]
        whole, budget = sum([loads[i] for i in movable]), surplus
        for i in movable:
            more = min(most - given[i], max(1, budget * loads[i] // whole), surplus)
            given[i] = given[i] + more
            surplus = surplus - more
    return np.array([most] + given)


def uneven(stream_key, amount, total, limit, slope):
    if amount == 2:
        one = jax.random.randint(stream_key, (), max(1, total - limit), min(limit, total - 1) + 1)
        return jnp.stack([one, total - one])
    sizes = jnp.asarray(length_profile(amount, total, limit, slope), jnp.int32)
    pairs = (amount - 1) // 2
    donor, receiver = sizes[1:1 + 2 * pairs:2], sizes[2:2 + 2 * pairs:2]
    room = jnp.minimum(donor - 1, limit - receiver)
    passed = jax.random.randint(jax.random.fold_in(stream_key, 1), (pairs,), 0, 1 << 20) % (room + 1)
    sizes = sizes.at[1:1 + 2 * pairs:2].set(donor - passed).at[2:2 + 2 * pairs:2].set(receiver + passed)
    return sizes[jax.random.permutation(jax.random.fold_in(stream_key, 2), amount)]


def gaussian(rng, extent, width, reach, cuts=(), kind=jnp.bfloat16):
    factor_of = block_scale(rng, extent, cuts, -0.22, 0.18) if cuts else 1.0
    entries = jax.random.normal(rng, extent, jnp.float32) * width * factor_of
    return jnp.minimum(jnp.maximum(entries, -reach), reach).astype(kind)


def setup_inputs(seed: int = 0, part: int = 0) -> dict:
    key_of = jax.random.split(jax.random.key(seed), 11)
    own_keys = jax.random.split(jax.random.fold_in(key_of[10], part), 11)
    alignment = draw_alignment(jax.random.fold_in(jax.random.fold_in(key_of[10], part), 71), part)
    seq_mask = draw_seq_mask(jax.random.fold_in(jax.random.fold_in(key_of[10], part), 71), part)
    pair_rep = gaussian(own_keys[2], (R, R, CZ), 1.0, 6.0, ((0, 4), (1, 4)), jnp.float32)
    chain_index = jnp.searchsorted(jnp.cumsum(uneven(own_keys[3], 4, R, R // 2, 0)), jnp.arange(R), side="right").astype(jnp.int32)
    rel_table = gaussian(key_of[4], (BINS, CZ), 0.5, 3.0, (), jnp.float32)
    w_factors = gaussian(key_of[5], (C, 2 * CO), C ** -0.5, 0.75)
    w_outer = gaussian(key_of[6], (CO * CO, CZ), (CO * CO) ** -0.5, 0.1875, (), jnp.float32)
    w_bias = gaussian(key_of[7], (CZ, HEADS), 0.25, 1.5, (), jnp.float32)
    w_attention = draw_w_attention(jax.random.fold_in(key_of[10], 71), part)
    w_output = gaussian(key_of[9], (HEADS * HD, C), (HEADS * HD) ** -0.5, 0.75)
    return {"alignment": alignment, "seq_mask": seq_mask, "pair_rep": pair_rep, "chain_index": chain_index, "rel_table": rel_table, "w_factors": w_factors, "w_outer": w_outer, "w_bias": w_bias, "w_attention": w_attention, "w_output": w_output}


EPSILON = 1e-05
PRECISE = lax.Precision.HIGHEST

def layer_norm(values):
    average = lax.optimization_barrier(jnp.mean(values, -1, keepdims=True))
    centred = values - average
    variance = lax.optimization_barrier(jnp.mean(centred * centred, -1, keepdims=True))
    return centred * lax.rsqrt(variance + EPSILON)

def reference(alignment, seq_mask, pair_rep, chain_index, rel_table, w_factors, w_outer, w_bias, w_attention, w_output):
    mask_float = seq_mask.astype(jnp.float32)
    normed = layer_norm(alignment).astype(jnp.bfloat16)
    flattened = normed.reshape(S * R, C)
    projected = jnp.dot(flattened, w_factors, preferred_element_type=jnp.float32).reshape(S, R, 2 * CO)
    left_factor = (projected[..., :CO] * mask_float[..., None]).astype(jnp.bfloat16)
    right_factor = (projected[..., CO:] * mask_float[..., None]).astype(jnp.bfloat16)
    counted = jnp.dot(mask_float.T, mask_float, precision=PRECISE, preferred_element_type=jnp.float32)
    right_wide = right_factor.astype(jnp.float32)
    left_blocks = left_factor.reshape(S, R // RES_DEV, RES_DEV, CO).transpose(1, 0, 2, 3)

    def outer_block(left_block):
        outer_sum = jnp.einsum('sic,sje->ijce', left_block.astype(jnp.float32), right_wide, precision=PRECISE)
        flat_outer = outer_sum.reshape(RES_DEV * R, CO * CO)
        return jnp.dot(flat_outer, w_outer, precision=PRECISE, preferred_element_type=jnp.float32).reshape(RES_DEV, R, CZ)
    update = lax.map(outer_block, left_blocks).reshape(R, R, CZ) / jnp.maximum(counted, 1.0)[..., None]
    positions = jnp.arange(R, dtype=jnp.int32)
    same_chain = chain_index[:, None] == chain_index[None, :]
    rel_bins = jnp.where(same_chain, jnp.clip(positions[:, None] - positions[None, :] + RELMAX, 0, 2 * RELMAX), 2 * RELMAX + 1).astype(jnp.int32)
    pair_next = pair_rep + rel_table[rel_bins] + update
    head_bias = jnp.dot(layer_norm(pair_next).reshape(R * R, CZ), w_bias, precision=PRECISE, preferred_element_type=jnp.float32)
    head_bias = head_bias.reshape(R, R, HEADS).transpose(2, 0, 1)
    inner_width = HEADS * HD
    features = jnp.dot(flattened, w_attention, preferred_element_type=jnp.float32).reshape(S, R, 4 * inner_width)
    queries = features[..., :inner_width].astype(jnp.bfloat16)
    keys = features[..., inner_width:2 * inner_width].astype(jnp.bfloat16)
    values = features[..., 2 * inner_width:3 * inner_width].astype(jnp.bfloat16)
    gate_logits = features[..., 3 * inner_width:]
    score_scale = 1.0 / math.sqrt(HD)

    def attend(block):
        query_block, key_block, value_block, gate_block, mask_block = block
        query_heads = query_block.astype(jnp.float32).reshape(SEQ_DEV, R, HEADS, HD)
        key_heads = key_block.astype(jnp.float32).reshape(SEQ_DEV, R, HEADS, HD)
        value_heads = value_block.astype(jnp.float32).reshape(SEQ_DEV, R, HEADS, HD)
        scores = jnp.einsum('bihd,bjhd->bhij', query_heads, key_heads, precision=PRECISE) * score_scale
        scores = scores + head_bias[None] + 1000000000.0 * (mask_block[:, None, None, :] - 1.0)
        row_max = lax.optimization_barrier(jnp.max(scores, -1, keepdims=True))
        weights = jnp.exp(scores - row_max)
        weights = (weights / lax.optimization_barrier(jnp.sum(weights, -1, keepdims=True))).astype(jnp.bfloat16)
        attended = jnp.einsum('bhij,bjhd->bihd', weights.astype(jnp.float32), value_heads, precision=PRECISE)
        attended = attended.reshape(SEQ_DEV, R, inner_width)
        return (jax.nn.sigmoid(gate_block) * attended).astype(jnp.bfloat16)
    groups = S // SEQ_DEV
    gated = lax.map(attend, (queries.reshape(groups, SEQ_DEV, R, inner_width), keys.reshape(groups, SEQ_DEV, R, inner_width), values.reshape(groups, SEQ_DEV, R, inner_width), gate_logits.reshape(groups, SEQ_DEV, R, inner_width), mask_float.reshape(groups, SEQ_DEV, R)))
    gated = gated.reshape(S * R, inner_width)
    alignment_next = alignment + jnp.dot(gated, w_output, preferred_element_type=jnp.float32).reshape(S, R, C)
    return (pair_next, alignment_next)
```

```python
import functools
import math

import jax
import jax.numpy as jnp
from jax import lax
from jax.experimental import pallas as pl
from jax.experimental.pallas import tpu as pltpu
from jax.sharding import PartitionSpec as P

EPSILON = 1e-05
PRECISE = lax.Precision.HIGHEST
MESH = pl.DeviceIdType.MESH
F32 = jnp.float32
BF16 = jnp.bfloat16
LANES = 128


def iota(shape, dim):
    return lax.broadcasted_iota(jnp.int32, shape, dim)


def dot(a, b, dims=((1,), (0,)), precision=None):
    return lax.dot_general(
        a, b, (dims, ((), ())), precision=precision, preferred_element_type=F32
    )


def layer_norm(values):
    average = jnp.mean(values, -1, keepdims=True)
    centred = values - average
    variance = jnp.mean(centred * centred, -1, keepdims=True)
    return centred * lax.rsqrt(variance + EPSILON)


def split(values):
    high = values.astype(BF16)
    return high, (values - high.astype(F32)).astype(BF16)


def kernel(
    n_seq,
    n_res,
    sizes,
    align_ref,
    mask_ref,
    pair_ref,
    chain_ref,
    table_ref,
    wf_ref,
    wo_ref,
    wb_ref,
    wa_ref,
    wout_ref,
    pair_out,
    align_out,
    x_scr,
    left_buf,
    right_buf,
    right_own,
    x_buf,
    mask_buf,
    bias_buf,
    bias_own,
    bias_scr,
    base_scr,
    wsplit,
    wa_diag,
    qk_scr,
    vg_scr,
    q_scr,
    gate_scr,
    outer_scr,
    lhs_high,
    lhs_low,
    att_scr,
    score_scr,
    send_l,
    recv_l,
    send_r,
    recv_r,
    send_x,
    recv_x,
    send_m,
    recv_m,
    send_b,
    recv_b,
):
    sd, rd, ch, cb, cz, co, heads, hd, bins = sizes
    inner = heads * hd
    ratio = rd // cb
    rows = sd * rd
    pairs = rd * cb
    residues = n_res * rd
    fl = rd * co
    q = lax.axis_index("seq")
    r = lax.axis_index("res")
    owner = q // ratio
    diagonal = (owner == r).astype(jnp.int32)

    barrier = pltpu.get_barrier_semaphore()
    seq_peers = [lax.rem(q + d, n_seq) for d in range(n_seq)]
    res_peers = [lax.rem(r + d, n_res) for d in range(n_res)]
    for d in range(1, n_seq):
        pl.semaphore_signal(
            barrier, inc=1, device_id={"seq": seq_peers[d], "res": r}, device_id_type=MESH
        )
    for d in range(1, n_res):
        pl.semaphore_signal(
            barrier, inc=1, device_id={"seq": q, "res": res_peers[d]}, device_id_type=MESH
        )
    for d in range(n_seq):

        def greet(d=d):
            pl.semaphore_signal(
                barrier, inc=1, device_id={"seq": seq_peers[d], "res": owner}, device_id_type=MESH
            )

        if d == 0:
            pl.when(owner != r)(greet)
        else:
            greet()

    normed = layer_norm(align_ref[...])
    x_scr[...] = normed
    half = rows // 2
    x_buf[r] = jnp.concatenate([normed[:half], normed[half:]], axis=1).astype(BF16)
    mask = mask_ref[...].astype(F32)
    eye = (iota((rd, rd), 0) == iota((rd, rd), 1)).astype(BF16)
    mask_turned = dot(eye, mask.astype(BF16), ((1,), (1,)))
    mask_wide = jnp.concatenate([mask_turned, jnp.zeros((rd, LANES - sd), F32)], axis=1)
    mask_buf[r] = mask_wide
    wf = wf_ref[...]
    wf_wide = jnp.concatenate([wf, wf], axis=1)
    per = LANES // co
    lane_block = iota((sd, LANES), 1) // co
    for g in range(rd // per):
        left = jnp.zeros((sd, LANES), F32)
        right = jnp.zeros((sd, LANES), F32)
        for m in range(per):
            i = g * per + m
            factor = dot(x_scr[pl.ds(i, sd, stride=rd), :].astype(BF16), wf_wide)
            factor = factor * mask[:, i : i + 1]
            left_at = (co * m) % LANES
            right_at = (co * m - co) % LANES
            left = jnp.where(lane_block == m, pltpu.roll(factor, left_at, 1) if left_at else factor, left)
            right = jnp.where(
                lane_block == m, pltpu.roll(factor, right_at, 1) if right_at else factor, right
            )
        left_buf[q, :, g * LANES : (g + 1) * LANES] = left.astype(BF16)
        right_own[:, g * LANES : (g + 1) * LANES] = right.astype(BF16)
    mask_pad = jnp.concatenate([mask, jnp.zeros((sd, LANES - rd), F32)], axis=1).astype(BF16)
    left_buf[q, :, fl : fl + LANES] = mask_pad
    right_own[:, fl : fl + LANES] = mask_pad

    pl.semaphore_wait(barrier, (n_seq - 1) + (n_res - 1) + ratio * n_res - diagonal)

    def right_copy(t, d):
        return pltpu.make_async_remote_copy(
            src_ref=right_own,
            dst_ref=right_buf.at[q],
            send_sem=send_r.at[t * n_res + d],
            recv_sem=recv_r.at[q],
            device_id={"seq": r * ratio + t, "res": res_peers[d]},
            device_id_type=MESH,
        )

    def left_copy(d):
        return pltpu.make_async_remote_copy(
            src_ref=left_buf.at[q],
            dst_ref=left_buf.at[q],
            send_sem=send_l.at[d],
            recv_sem=recv_l.at[d],
            device_id={"seq": seq_peers[d], "res": r},
            device_id_type=MESH,
        )

    def x_copy(d):
        return pltpu.make_async_remote_copy(
            src_ref=x_buf.at[r],
            dst_ref=x_buf.at[r],
            send_sem=send_x.at[d],
            recv_sem=recv_x.at[d],
            device_id={"seq": q, "res": res_peers[d]},
            device_id_type=MESH,
        )

    def mask_copy(d):
        return pltpu.make_async_remote_copy(
            src_ref=mask_buf.at[r],
            dst_ref=mask_buf.at[r],
            send_sem=send_m.at[d],
            recv_sem=recv_m.at[d],
            device_id={"seq": q, "res": res_peers[d]},
            device_id_type=MESH,
        )

    def each_right(action):
        for t in range(ratio):
            for d in range(n_res):
                if d == 0:
                    pl.when(r * ratio + t != q)(functools.partial(action, t, d))
                else:
                    action(t, d)

    each_right(lambda t, d: right_copy(t, d).start())
    for d in range(1, n_seq):
        left_copy(d).start()
    for d in range(1, n_res):
        x_copy(d).start()
        mask_copy(d).start()

    @pl.when(owner == r)
    def _():
        right_buf[q] = right_own[...]

    wo_high, wo_low = split(wo_ref[...])
    wsplit[:, :cz] = wo_high
    wsplit[:, cz:] = wo_low
    wa_diag[...] = jnp.zeros_like(wa_diag)
    wa_diag[:ch, : 4 * inner] = wa_ref[...]
    wa_diag[ch:, 4 * inner :] = wa_ref[...]

    row = iota((rd, LANES), 0)
    lane = iota((rd, LANES), 1)
    reach = (bins - 2) // 2
    row_chain = jnp.zeros((rd, LANES), jnp.int32)
    for i in range(rd):
        row_chain = jnp.where(row == i, chain_ref[r * rd + i], row_chain)
    tab_high, tab_low = split(
        jnp.concatenate([table_ref[...], jnp.zeros((LANES - bins, cz), F32)], axis=0)
    )
    hot = []
    for j in range(cb):
        column = q * cb + j
        bin_ = jnp.where(
            row_chain == chain_ref[column],
            jnp.clip(row + r * rd - column + reach, 0, 2 * reach),
            2 * reach + 1,
        )
        hot.append(jnp.where(lane == bin_, 1.0, 0.0).astype(BF16))
    hot = jnp.concatenate(hot, axis=0)
    relative = dot(hot, tab_high) + dot(hot, tab_low)
    for j in range(cb):
        base_scr[j * rd : (j + 1) * rd] = (
            pair_ref[pl.ds(j, rd, stride=cb), :] + relative[j * rd : (j + 1) * rd]
        )

    spread = (iota((heads, LANES), 1) // rd == iota((heads, LANES), 0)).astype(F32)
    wb_high, wb_low = split(dot(wb_ref[...], spread, precision=PRECISE))
    wb_both = jnp.concatenate([wb_high, wb_low], axis=1)

    def project(block):
        features = dot(x_buf[block], wa_diag[...])
        for part in range(2):
            at = 4 * inner * part
            qk_scr[block, part * half : (part + 1) * half] = features[:, at : at + LANES].astype(BF16)
            vg_scr[block, part * half : (part + 1) * half] = features[
                :, at + LANES : at + 2 * LANES
            ].astype(BF16)
        return features

    own = project(r)
    for part in range(2):
        at = 4 * inner * part
        place = slice(part * half, (part + 1) * half)
        q_scr[place] = pltpu.roll(own[:, at : at + LANES], inner, 1).astype(BF16)
        gate_scr[place] = jax.nn.sigmoid(
            pltpu.roll(own[:, at + LANES : at + 2 * LANES], inner, 1)
        )

    for d in range(1, n_seq):
        left_copy(d).wait_recv()
    for source in range(n_seq):

        def arrive(source=source):
            pltpu.make_async_remote_copy(
                src_ref=right_own,
                dst_ref=right_buf.at[source],
                send_sem=send_r.at[0],
                recv_sem=recv_r.at[source],
                device_id={"seq": source, "res": owner},
                device_id_type=MESH,
            ).wait_recv()

        pl.when(jnp.logical_or(owner != r, q != source))(arrive)

    left_all = left_buf[:, :, :fl].reshape(n_seq * sd, fl)
    block = iota((rd, LANES), 1) // co
    block_tall = jnp.concatenate([block] * (co // per), axis=0)
    for g in range(cb // per):
        at = g * LANES
        if ratio > 1:
            at = pl.multiple_of(lax.rem(q, ratio) * (cb * co) + g * LANES, LANES)
        right_part = right_buf[:, :, pl.ds(at, LANES)].reshape(n_seq * sd, LANES)
        outer_scr[g] = dot(left_all, right_part, ((0,), (0,)))
        tall = [
            jnp.concatenate(
                [outer_scr[g, pl.ds(per * k + m, rd, stride=co), :] for k in range(co // per)], axis=0
            )
            for m in range(per)
        ]
        for jj in range(per):
            total = None
            for m in range(per):
                shift = (co * (m - jj)) % LANES
                moved = pltpu.roll(tall[m], shift, 1) if shift else tall[m]
                total = moved if total is None else jnp.where(block_tall == m, moved, total)
            high, low = split(total)
            place = slice((g * per + jj) * rd, (g * per + jj + 1) * rd)
            for k in range(co // per):
                lhs_high[place, k * LANES : (k + 1) * LANES] = high[k * rd : (k + 1) * rd]
                lhs_low[place, k * LANES : (k + 1) * LANES] = low[k * rd : (k + 1) * rd]
    both = dot(lhs_high[...], wsplit[...])
    update = both[:, :cz] + both[:, cz:] + dot(lhs_low[...], wsplit[:, :cz])
    counted = dot(
        left_buf[:, :, fl : fl + LANES].reshape(n_seq * sd, LANES),
        right_buf[:, :, fl : fl + LANES].reshape(n_seq * sd, LANES),
        ((0,), (0,)),
    )[:rd]
    if ratio > 1:
        counted = pltpu.roll(counted, LANES - lax.rem(q, ratio) * cb, 1)
    scale = 1.0 / jnp.maximum(counted, 1.0)
    scale = jnp.concatenate(
        [jnp.broadcast_to(scale[:, j : j + 1], (rd, LANES)) for j in range(cb)], axis=0
    )
    pair_next = base_scr[...] + update * scale
    for j in range(cb):
        pair_out[pl.ds(j, rd, stride=cb), :] = pair_next[j * rd : (j + 1) * rd]
    n_high, n_low = split(layer_norm(pair_next))
    both = dot(n_high, wb_both)
    head = both[:, :LANES] + both[:, LANES:] + dot(n_low, wb_high)
    keep = iota((pairs, LANES), 0) % rd == iota((pairs, LANES), 1) % rd
    head = jnp.where(keep, head, 0.0).reshape(cb, rd, LANES)
    bias_own[:cb] = jnp.sum(head, axis=1)

    def bias_copy(d):
        return pltpu.make_async_remote_copy(
            src_ref=bias_own,
            dst_ref=bias_buf.at[q],
            send_sem=send_b.at[d],
            recv_sem=recv_b.at[d],
            device_id={"seq": seq_peers[d], "res": r},
            device_id_type=MESH,
        )

    for d in range(1, n_seq):
        bias_copy(d).start()
    bias_buf[q] = bias_own[...]

    for d in range(1, n_res):
        x_copy(d).wait_recv()
        mask_copy(d).wait_recv()
    for d in range(1, n_res):
        project(lax.rem(r + n_res - d, n_res))
    wide = heads * rd
    wide_row = iota((wide, LANES), 0) // rd
    wide_lane = iota((wide, LANES), 1)
    query_mask = jnp.where((wide_lane - inner) // hd == wide_row, 1.0, 0.0)
    query_mask = jnp.where(wide_lane >= inner, query_mask, 0.0).astype(BF16)
    out_mask = wide_lane // hd == wide_row
    score_scale = 1.0 / math.sqrt(hd)
    for s in range(sd):
        at = slice(s * rd, (s + 1) * rd)
        keys = qk_scr[:, at].reshape(residues, LANES)
        queries = jnp.concatenate([q_scr[at]] * heads, axis=0) * query_mask
        score_scr[s] = dot(keys, queries, ((1,), (1,))) * score_scale
    mask_bias = 1000000000.0 * (mask_buf[...].reshape(residues, LANES) - 1.0)

    for d in range(1, n_seq):
        bias_copy(d).wait_recv()
    for j in range(n_seq):
        bias_scr[j * cb : (j + 1) * cb] = bias_buf[j, :cb]
    bias = bias_scr[...]
    for s in range(sd):
        at = slice(s * rd, (s + 1) * rd)
        scores = score_scr[s] + bias + mask_bias[:, s : s + 1]
        weights = jnp.exp(scores - jnp.max(scores, 0, keepdims=True))
        weights = (weights * (1.0 / jnp.sum(weights, 0, keepdims=True))).astype(BF16)
        values = vg_scr[:, at].reshape(residues, LANES)
        mixed = jnp.where(out_mask, dot(weights, values, ((0,), (0,))), 0.0)
        att_scr[at] = jnp.sum(mixed.reshape(heads, rd, LANES), axis=0)
    gated = (gate_scr[...] * att_scr[...]).astype(BF16)[:, :inner]
    align_out[...] = align_ref[...] + dot(gated, wout_ref[...])

    each_right(lambda t, d: right_copy(t, d).wait_send())
    for d in range(1, n_seq):
        left_copy(d).wait_send()
        bias_copy(d).wait_send()
    for d in range(1, n_res):
        x_copy(d).wait_send()
        mask_copy(d).wait_send()


def solution(mesh):
    n_seq, n_res = mesh.shape["seq"], mesh.shape["res"]

    def body(align, mask, pair, chain, table, w_factors, w_outer, w_bias, w_attention, w_output):
        sd, rd, ch = align.shape
        cb, cz = pair.shape[1:]
        co = w_factors.shape[1] // 2
        heads = w_bias.shape[1]
        inner = w_attention.shape[1] // 4
        bins = table.shape[0]
        rows, pairs, residues = sd * rd, rd * cb, n_res * rd
        fl = rd * co
        per = LANES // co
        slot = max(cb, 8)
        sizes = (sd, rd, ch, cb, cz, co, heads, inner // heads, bins)
        vmem = pl.BlockSpec(memory_space=pltpu.VMEM)
        smem = pl.BlockSpec(memory_space=pltpu.SMEM)
        dma = pltpu.SemaphoreType.DMA
        pair_next, align_next = pl.pallas_call(
            functools.partial(kernel, n_seq, n_res, sizes),
            out_shape=(
                jax.ShapeDtypeStruct((pairs, cz), F32),
                jax.ShapeDtypeStruct((rows, ch), F32),
            ),
            in_specs=[vmem, vmem, vmem, smem] + [vmem] * 6,
            out_specs=(vmem, vmem),
            scratch_shapes=[
                pltpu.VMEM((rows, ch), F32),
                pltpu.VMEM((n_seq, sd, fl + LANES), BF16),
                pltpu.VMEM((n_seq, sd, fl + LANES), BF16),
                pltpu.VMEM((sd, fl + LANES), BF16),
                pltpu.VMEM((n_res, rows // 2, 2 * ch), BF16),
                pltpu.VMEM((n_res, rd, LANES), F32),
                pltpu.VMEM((n_seq, slot, LANES), F32),
                pltpu.VMEM((slot, LANES), F32),
                pltpu.VMEM((residues, LANES), F32),
                pltpu.VMEM((pairs, cz), F32),
                pltpu.VMEM((co * co, 2 * cz), BF16),
                pltpu.VMEM((2 * ch, 8 * inner), BF16),
                pltpu.VMEM((n_res, rows, LANES), BF16),
                pltpu.VMEM((n_res, rows, LANES), BF16),
                pltpu.VMEM((rows, LANES), BF16),
                pltpu.VMEM((rows, LANES), F32),
                pltpu.VMEM((cb // per, fl, LANES), F32),
                pltpu.VMEM((pairs, co * co), BF16),
                pltpu.VMEM((pairs, co * co), BF16),
                pltpu.VMEM((rows, LANES), F32),
                pltpu.VMEM((sd, residues, LANES), F32),
                dma((n_seq,)),
                dma((n_seq,)),
                dma((rd // cb * n_res,)),
                dma((n_seq,)),
                dma((n_res,)),
                dma((n_res,)),
                dma((n_res,)),
                dma((n_res,)),
                dma((n_seq,)),
                dma((n_seq,)),
            ],
            compiler_params=pltpu.CompilerParams(
                collective_id=0, has_side_effects=True, vmem_limit_bytes=48 * 1024 * 1024
            ),
        )(
            align.reshape(rows, ch),
            mask,
            pair.reshape(pairs, cz),
            chain,
            table,
            w_factors,
            w_outer,
            w_bias,
            w_attention,
            w_output,
        )
        return pair_next.reshape(rd, cb, cz), align_next.reshape(sd, rd, ch)

    in_specs = (
        P(("groups", "seq"), "res", None),
        P(("groups", "seq"), "res"),
        P(("groups", "res"), "seq", None),
        P("groups"),
        P(),
        P(),
        P(),
        P(),
        P(),
        P(),
    )
    out_specs = (P(("groups", "res"), "seq", None), P(("groups", "seq"), "res", None))
    return jax.shard_map(body, mesh=mesh, in_specs=in_specs, out_specs=out_specs, check_vma=False)
```

```python
import functools
import math

import jax
import jax.numpy as jnp
from jax import lax
from jax.experimental import pallas as pl
from jax.experimental.pallas import tpu as pltpu
from jax.sharding import PartitionSpec as P

EPSILON = 1e-05
PRECISE = lax.Precision.HIGHEST
MESH = pl.DeviceIdType.MESH
F32 = jnp.float32
BF16 = jnp.bfloat16
LANES = 128


def iota(shape, dim):
    return lax.broadcasted_iota(jnp.int32, shape, dim)


def dot(a, b, dims=((1,), (0,)), precision=None):
    return lax.dot_general(
        a, b, (dims, ((), ())), precision=precision, preferred_element_type=F32
    )


def layer_norm(values):
    average = jnp.mean(values, -1, keepdims=True)
    centred = values - average
    variance = jnp.mean(centred * centred, -1, keepdims=True)
    return centred * lax.rsqrt(variance + EPSILON)


def split(values):
    high = values.astype(BF16)
    return high, (values - high.astype(F32)).astype(BF16)


def kernel(
    n_seq,
    n_res,
    sizes,
    align_hbm,
    mask_hbm,
    pair_hbm,
    chain_hbm,
    table_hbm,
    wf_hbm,
    wo_hbm,
    wb_hbm,
    wa_hbm,
    wout_hbm,
    pair_out,
    align_out,
    align_ref,
    mask_ref,
    pair_ref,
    chain_ref,
    table_ref,
    wf_ref,
    wo_ref,
    wb_ref,
    wa_ref,
    wout_ref,
    load_sem,
    x_scr,
    left_buf,
    right_buf,
    right_own,
    x_buf,
    mask_buf,
    bias_buf,
    bias_own,
    bias_scr,
    base_scr,
    wsplit,
    wa_diag,
    qk_scr,
    vg_scr,
    q_scr,
    gate_scr,
    outer_scr,
    lhs_high,
    lhs_low,
    att_scr,
    score_scr,
    send_l,
    recv_l,
    send_r,
    recv_r,
    send_x,
    recv_x,
    send_m,
    recv_m,
    send_b,
    recv_b,
):
    sd, rd, ch, cb, cz, co, heads, hd, bins = sizes
    inner = heads * hd
    ratio = rd // cb
    rows = sd * rd
    pairs = rd * cb
    residues = n_res * rd
    fl = rd * co
    q = lax.axis_index("seq")
    r = lax.axis_index("res")
    owner = q // ratio
    diagonal = (owner == r).astype(jnp.int32)

    loads = [
        pltpu.make_async_copy(source, target, load_sem.at[index])
        for index, (source, target) in enumerate(
            (
                (align_hbm, align_ref),
                (mask_hbm, mask_ref),
                (wf_hbm, wf_ref),
                (wo_hbm, wo_ref),
                (wa_hbm, wa_ref),
                (chain_hbm, chain_ref),
                (table_hbm, table_ref),
                (pair_hbm, pair_ref),
                (wb_hbm, wb_ref),
                (wout_hbm, wout_ref),
            )
        )
    ]
    for load in loads:
        load.start()

    barrier = pltpu.get_barrier_semaphore()
    seq_peers = [lax.rem(q + d, n_seq) for d in range(n_seq)]
    res_peers = [lax.rem(r + d, n_res) for d in range(n_res)]
    for d in range(1, n_seq):
        pl.semaphore_signal(
            barrier, inc=1, device_id={"seq": seq_peers[d], "res": r}, device_id_type=MESH
        )
    for d in range(1, n_res):
        pl.semaphore_signal(
            barrier, inc=1, device_id={"seq": q, "res": res_peers[d]}, device_id_type=MESH
        )
    for d in range(n_seq):

        def greet(d=d):
            pl.semaphore_signal(
                barrier, inc=1, device_id={"seq": seq_peers[d], "res": owner}, device_id_type=MESH
            )

        if d == 0:
            pl.when(owner != r)(greet)
        else:
            greet()

    for load in loads[:3]:
        load.wait()
    normed = layer_norm(align_ref[...])
    x_scr[...] = normed
    half = rows // 2
    x_buf[r] = jnp.concatenate([normed[:half], normed[half:]], axis=1).astype(BF16)
    mask_turned = mask_ref[...].astype(F32)
    eye = (iota((rd, rd), 0) == iota((rd, rd), 1)).astype(BF16)
    mask = dot(mask_turned.astype(BF16), eye, ((0,), (0,)))
    mask_wide = jnp.concatenate([mask_turned, jnp.zeros((rd, LANES - sd), F32)], axis=1)
    mask_buf[r] = mask_wide
    wf = wf_ref[...]
    wf_wide = jnp.concatenate([wf, wf], axis=1)
    per = LANES // co
    lane_block = iota((sd, LANES), 1) // co
    for g in range(rd // per):
        left = jnp.zeros((sd, LANES), F32)
        right = jnp.zeros((sd, LANES), F32)
        for m in range(per):
            i = g * per + m
            factor = dot(x_scr[pl.ds(i, sd, stride=rd), :].astype(BF16), wf_wide)
            factor = factor * mask[:, i : i + 1]
            left_at = (co * m) % LANES
            right_at = (co * m - co) % LANES
            left = jnp.where(lane_block == m, pltpu.roll(factor, left_at, 1) if left_at else factor, left)
            right = jnp.where(
                lane_block == m, pltpu.roll(factor, right_at, 1) if right_at else factor, right
            )
        left_buf[q, :, g * LANES : (g + 1) * LANES] = left.astype(BF16)
        right_own[:, g * LANES : (g + 1) * LANES] = right.astype(BF16)
    mask_pad = jnp.concatenate([mask, jnp.zeros((sd, LANES - rd), F32)], axis=1).astype(BF16)
    left_buf[q, :, fl : fl + LANES] = mask_pad
    right_own[:, fl : fl + LANES] = mask_pad

    pl.semaphore_wait(barrier, (n_seq - 1) + (n_res - 1) + ratio * n_res - diagonal)

    def right_copy(t, d):
        return pltpu.make_async_remote_copy(
            src_ref=right_own,
            dst_ref=right_buf.at[q],
            send_sem=send_r.at[t * n_res + d],
            recv_sem=recv_r.at[q],
            device_id={"seq": r * ratio + t, "res": res_peers[d]},
            device_id_type=MESH,
        )

    def left_copy(d):
        return pltpu.make_async_remote_copy(
            src_ref=left_buf.at[q],
            dst_ref=left_buf.at[q],
            send_sem=send_l.at[d],
            recv_sem=recv_l.at[d],
            device_id={"seq": seq_peers[d], "res": r},
            device_id_type=MESH,
        )

    def x_copy(d):
        return pltpu.make_async_remote_copy(
            src_ref=x_buf.at[r],
            dst_ref=x_buf.at[r],
            send_sem=send_x.at[d],
            recv_sem=recv_x.at[d],
            device_id={"seq": q, "res": res_peers[d]},
            device_id_type=MESH,
        )

    def mask_copy(d):
        return pltpu.make_async_remote_copy(
            src_ref=mask_buf.at[r],
            dst_ref=mask_buf.at[r],
            send_sem=send_m.at[d],
            recv_sem=recv_m.at[d],
            device_id={"seq": q, "res": res_peers[d]},
            device_id_type=MESH,
        )

    def each_right(action):
        for t in range(ratio):
            for d in range(n_res):
                if d == 0:
                    pl.when(r * ratio + t != q)(functools.partial(action, t, d))
                else:
                    action(t, d)

    each_right(lambda t, d: right_copy(t, d).start())
    for d in range(1, n_seq):
        left_copy(d).start()
    for d in range(1, n_res):
        x_copy(d).start()
        mask_copy(d).start()

    @pl.when(owner == r)
    def _():
        right_buf[q] = right_own[...]

    for load in loads[3:]:
        load.wait()
    wo_high, wo_low = split(wo_ref[...])
    wsplit[:, :cz] = wo_high
    wsplit[:, cz:] = wo_low
    wa_diag[...] = jnp.zeros_like(wa_diag)
    wa_diag[:ch, : 4 * inner] = wa_ref[...]
    wa_diag[ch:, 4 * inner :] = wa_ref[...]

    row = iota((rd, LANES), 0)
    lane = iota((rd, LANES), 1)
    reach = (bins - 2) // 2
    row_chain = jnp.zeros((rd, LANES), jnp.int32)
    for i in range(rd):
        row_chain = jnp.where(row == i, chain_ref[r * rd + i], row_chain)
    tab_high, tab_low = split(
        jnp.concatenate([table_ref[...], jnp.zeros((LANES - bins, cz), F32)], axis=0)
    )
    hot = []
    for j in range(cb):
        column = q * cb + j
        bin_ = jnp.where(
            row_chain == chain_ref[column],
            jnp.clip(row + r * rd - column + reach, 0, 2 * reach),
            2 * reach + 1,
        )
        hot.append(jnp.where(lane == bin_, 1.0, 0.0).astype(BF16))
    hot = jnp.concatenate(hot, axis=0)
    relative = dot(hot, tab_high) + dot(hot, tab_low)
    for j in range(cb):
        base_scr[j * rd : (j + 1) * rd] = (
            pair_ref[pl.ds(j, rd, stride=cb), :] + relative[j * rd : (j + 1) * rd]
        )

    spread = (iota((heads, LANES), 1) // rd == iota((heads, LANES), 0)).astype(F32)
    wb_high, wb_low = split(dot(wb_ref[...], spread, ((0,), (0,)), PRECISE))
    wb_both = jnp.concatenate([wb_high, wb_low], axis=1)

    def project(block):
        features = dot(x_buf[block], wa_diag[...])
        for part in range(2):
            at = 4 * inner * part
            qk_scr[block, part * half : (part + 1) * half] = features[:, at : at + LANES].astype(BF16)
            vg_scr[block, part * half : (part + 1) * half] = features[
                :, at + LANES : at + 2 * LANES
            ].astype(BF16)
        return features

    own = project(r)
    for part in range(2):
        at = 4 * inner * part
        place = slice(part * half, (part + 1) * half)
        q_scr[place] = pltpu.roll(own[:, at : at + LANES], inner, 1).astype(BF16)
        gate_scr[place] = jax.nn.sigmoid(
            pltpu.roll(own[:, at + LANES : at + 2 * LANES], inner, 1)
        )

    for d in range(1, n_seq):
        left_copy(d).wait_recv()
    for source in range(n_seq):

        def arrive(source=source):
            pltpu.make_async_remote_copy(
                src_ref=right_own,
                dst_ref=right_buf.at[source],
                send_sem=send_r.at[0],
                recv_sem=recv_r.at[source],
                device_id={"seq": source, "res": owner},
                device_id_type=MESH,
            ).wait_recv()

        pl.when(jnp.logical_or(owner != r, q != source))(arrive)

    left_all = left_buf[:, :, :fl].reshape(n_seq * sd, fl)
    block = iota((rd, LANES), 1) // co
    block_tall = jnp.concatenate([block] * (co // per), axis=0)
    for g in range(cb // per):
        at = g * LANES
        if ratio > 1:
            at = pl.multiple_of(lax.rem(q, ratio) * (cb * co) + g * LANES, LANES)
        right_part = right_buf[:, :, pl.ds(at, LANES)].reshape(n_seq * sd, LANES)
        outer_scr[g] = dot(left_all, right_part, ((0,), (0,)))
        tall = [
            jnp.concatenate(
                [outer_scr[g, pl.ds(per * k + m, rd, stride=co), :] for k in range(co // per)], axis=0
            )
            for m in range(per)
        ]
        for jj in range(per):
            total = None
            for m in range(per):
                shift = (co * (m - jj)) % LANES
                moved = pltpu.roll(tall[m], shift, 1) if shift else tall[m]
                total = moved if total is None else jnp.where(block_tall == m, moved, total)
            high, low = split(total)
            place = slice((g * per + jj) * rd, (g * per + jj + 1) * rd)
            for k in range(co // per):
                lhs_high[place, k * LANES : (k + 1) * LANES] = high[k * rd : (k + 1) * rd]
                lhs_low[place, k * LANES : (k + 1) * LANES] = low[k * rd : (k + 1) * rd]
    both = dot(lhs_high[...], wsplit[...])
    update = both[:, :cz] + both[:, cz:] + dot(lhs_low[...], wsplit[:, :cz])
    counted = dot(
        left_buf[:, :, fl : fl + LANES].reshape(n_seq * sd, LANES),
        right_buf[:, :, fl : fl + LANES].reshape(n_seq * sd, LANES),
        ((0,), (0,)),
    )[:rd]
    if ratio > 1:
        counted = pltpu.roll(counted, LANES - lax.rem(q, ratio) * cb, 1)
    scale = 1.0 / jnp.maximum(counted, 1.0)
    scale = jnp.concatenate(
        [jnp.broadcast_to(scale[:, j : j + 1], (rd, LANES)) for j in range(cb)], axis=0
    )
    pair_next = base_scr[...] + update * scale
    for j in range(cb):
        pair_out[pl.ds(j, rd, stride=cb), :] = pair_next[j * rd : (j + 1) * rd]
    n_high, n_low = split(layer_norm(pair_next))
    both = dot(n_high, wb_both)
    head = both[:, :LANES] + both[:, LANES:] + dot(n_low, wb_high)
    keep = iota((pairs, LANES), 0) % rd == iota((pairs, LANES), 1) % rd
    head = jnp.where(keep, head, 0.0).reshape(cb, rd, LANES)
    bias_own[:cb] = jnp.sum(head, axis=1)

    def bias_copy(d):
        return pltpu.make_async_remote_copy(
            src_ref=bias_own,
            dst_ref=bias_buf.at[q],
            send_sem=send_b.at[d],
            recv_sem=recv_b.at[d],
            device_id={"seq": seq_peers[d], "res": r},
            device_id_type=MESH,
        )

    for d in range(1, n_seq):
        bias_copy(d).start()
    bias_buf[q] = bias_own[...]

    for d in range(1, n_res):
        x_copy(d).wait_recv()
        mask_copy(d).wait_recv()
    for d in range(1, n_res):
        project(lax.rem(r + n_res - d, n_res))
    wide = heads * rd
    wide_row = iota((wide, LANES), 0) // rd
    wide_lane = iota((wide, LANES), 1)
    query_mask = jnp.where((wide_lane - inner) // hd == wide_row, 1.0, 0.0)
    query_mask = jnp.where(wide_lane >= inner, query_mask, 0.0).astype(BF16)
    out_mask = wide_lane // hd == wide_row
    score_scale = 1.0 / math.sqrt(hd)
    for s in range(sd):
        at = slice(s * rd, (s + 1) * rd)
        keys = qk_scr[:, at].reshape(residues, LANES)
        queries = jnp.concatenate([q_scr[at]] * heads, axis=0) * query_mask
        score_scr[s] = dot(keys, queries, ((1,), (1,))) * score_scale
    mask_bias = 1000000000.0 * (mask_buf[...].reshape(residues, LANES) - 1.0)

    for d in range(1, n_seq):
        bias_copy(d).wait_recv()
    for j in range(n_seq):
        bias_scr[j * cb : (j + 1) * cb] = bias_buf[j, :cb]
    bias = bias_scr[...]
    for s in range(sd):
        at = slice(s * rd, (s + 1) * rd)
        scores = score_scr[s] + bias + mask_bias[:, s : s + 1]
        weights = jnp.exp(scores - jnp.max(scores, 0, keepdims=True))
        weights = (weights * (1.0 / jnp.sum(weights, 0, keepdims=True))).astype(BF16)
        values = vg_scr[:, at].reshape(residues, LANES)
        mixed = jnp.where(out_mask, dot(weights, values, ((0,), (0,))), 0.0)
        att_scr[at] = jnp.sum(mixed.reshape(heads, rd, LANES), axis=0)
    gated = (gate_scr[...] * att_scr[...]).astype(BF16)[:, :inner]
    align_out[...] = align_ref[...] + dot(gated, wout_ref[...])

    each_right(lambda t, d: right_copy(t, d).wait_send())
    for d in range(1, n_seq):
        left_copy(d).wait_send()
        bias_copy(d).wait_send()
    for d in range(1, n_res):
        x_copy(d).wait_send()
        mask_copy(d).wait_send()


def solution(mesh):
    n_seq, n_res = mesh.shape["seq"], mesh.shape["res"]

    def body(align, mask, pair, chain, table, w_factors, w_outer, w_bias, w_attention, w_output):
        sd, rd, ch = align.shape
        cb, cz = pair.shape[1:]
        co = w_factors.shape[1] // 2
        heads = w_bias.shape[1]
        inner = w_attention.shape[1] // 4
        bins = table.shape[0]
        rows, pairs, residues = sd * rd, rd * cb, n_res * rd
        fl = rd * co
        per = LANES // co
        slot = max(cb, 8)
        sizes = (sd, rd, ch, cb, cz, co, heads, inner // heads, bins)
        vmem = pl.BlockSpec(memory_space=pltpu.VMEM)
        hbm = pl.BlockSpec(memory_space=pltpu.HBM)
        dma = pltpu.SemaphoreType.DMA
        pair_next, align_next = pl.pallas_call(
            functools.partial(kernel, n_seq, n_res, sizes),
            out_shape=(
                jax.ShapeDtypeStruct((pairs, cz), F32),
                jax.ShapeDtypeStruct((rows, ch), F32),
            ),
            in_specs=[hbm] * 10,
            out_specs=(vmem, vmem),
            scratch_shapes=[
                pltpu.VMEM((rows, ch), F32),
                pltpu.VMEM((rd, sd), jnp.int32),
                pltpu.VMEM((pairs, cz), F32),
                pltpu.SMEM((residues,), jnp.int32),
                pltpu.VMEM((bins, cz), F32),
                pltpu.VMEM((ch, 2 * co), BF16),
                pltpu.VMEM((co * co, cz), F32),
                pltpu.VMEM((heads, cz), F32),
                pltpu.VMEM((ch, 4 * inner), BF16),
                pltpu.VMEM((inner, ch), BF16),
                dma((10,)),
                pltpu.VMEM((rows, ch), F32),
                pltpu.VMEM((n_seq, sd, fl + LANES), BF16),
                pltpu.VMEM((n_seq, sd, fl + LANES), BF16),
                pltpu.VMEM((sd, fl + LANES), BF16),
                pltpu.VMEM((n_res, rows // 2, 2 * ch), BF16),
                pltpu.VMEM((n_res, rd, LANES), F32),
                pltpu.VMEM((n_seq, slot, LANES), F32),
                pltpu.VMEM((slot, LANES), F32),
                pltpu.VMEM((residues, LANES), F32),
                pltpu.VMEM((pairs, cz), F32),
                pltpu.VMEM((co * co, 2 * cz), BF16),
                pltpu.VMEM((2 * ch, 8 * inner), BF16),
                pltpu.VMEM((n_res, rows, LANES), BF16),
                pltpu.VMEM((n_res, rows, LANES), BF16),
                pltpu.VMEM((rows, LANES), BF16),
                pltpu.VMEM((rows, LANES), F32),
                pltpu.VMEM((cb // per, fl, LANES), F32),
                pltpu.VMEM((pairs, co * co), BF16),
                pltpu.VMEM((pairs, co * co), BF16),
                pltpu.VMEM((rows, LANES), F32),
                pltpu.VMEM((sd, residues, LANES), F32),
                dma((n_seq,)),
                dma((n_seq,)),
                dma((rd // cb * n_res,)),
                dma((n_seq,)),
                dma((n_res,)),
                dma((n_res,)),
                dma((n_res,)),
                dma((n_res,)),
                dma((n_seq,)),
                dma((n_seq,)),
            ],
            compiler_params=pltpu.CompilerParams(
                collective_id=0, has_side_effects=True, vmem_limit_bytes=64 * 1024 * 1024 - 65536
            ),
        )(
            align.reshape(rows, ch),
            mask.T,
            pair.reshape(pairs, cz),
            chain,
            table,
            w_factors,
            w_outer,
            w_bias.T,
            w_attention,
            w_output,
        )
        return pair_next.reshape(rd, cb, cz), align_next.reshape(sd, rd, ch)

    in_specs = (
        P(("groups", "seq"), "res", None),
        P(("groups", "seq"), "res"),
        P(("groups", "res"), "seq", None),
        P("groups"),
        P(),
        P(),
        P(),
        P(),
        P(),
        P(),
    )
    out_specs = (P(("groups", "res"), "seq", None), P(("groups", "seq"), "res", None))
    return jax.shard_map(body, mesh=mesh, in_specs=in_specs, out_specs=out_specs, check_vma=False)
```

```python
import functools
import math

import jax
import jax.numpy as jnp
from jax import lax
from jax.experimental import pallas as pl
from jax.experimental.pallas import tpu as pltpu
from jax.sharding import PartitionSpec as P

EPSILON = 1e-05
PRECISE = lax.Precision.HIGHEST
MESH = pl.DeviceIdType.MESH
F32 = jnp.float32
BF16 = jnp.bfloat16
LANES = 128


def iota(shape, dim):
    return lax.broadcasted_iota(jnp.int32, shape, dim)


def dot(a, b, dims=((1,), (0,)), precision=None):
    return lax.dot_general(
        a, b, (dims, ((), ())), precision=precision, preferred_element_type=F32
    )


def layer_norm(values):
    average = jnp.mean(values, -1, keepdims=True)
    centred = values - average
    variance = jnp.mean(centred * centred, -1, keepdims=True)
    return centred * lax.rsqrt(variance + EPSILON)


def split(values):
    high = values.astype(BF16)
    return high, (values - high.astype(F32)).astype(BF16)


def kernel(
    n_seq,
    n_res,
    sizes,
    align_hbm,
    mask_hbm,
    pair_hbm,
    chain_hbm,
    table_hbm,
    wf_hbm,
    wo_hbm,
    wb_hbm,
    wa_hbm,
    wout_hbm,
    pair_out,
    align_out,
    align_ref,
    mask_ref,
    pair_ref,
    chain_ref,
    table_ref,
    wf_ref,
    wo_ref,
    wb_ref,
    wa_ref,
    wout_ref,
    load_sem,
    x_scr,
    left_buf,
    right_buf,
    right_own,
    x_buf,
    mask_buf,
    bias_buf,
    bias_own,
    bias_scr,
    base_scr,
    wsplit,
    wa_diag,
    qk_scr,
    vg_scr,
    q_scr,
    gate_scr,
    outer_scr,
    lhs_high,
    lhs_low,
    att_scr,
    score_scr,
    send_l,
    recv_l,
    send_r,
    send_f,
    recv_r,
    send_x,
    recv_x,
    send_m,
    recv_m,
    send_b,
    recv_b,
):
    sd, rd, ch, cb, cz, co, heads, hd, bins = sizes
    inner = heads * hd
    ratio = rd // cb
    rows = sd * rd
    pairs = rd * cb
    residues = n_res * rd
    fl = rd * co
    q = lax.axis_index("seq")
    r = lax.axis_index("res")
    owner = q // ratio
    relay = lax.rem(q, n_res)
    own_slot = jnp.logical_and(owner == r, relay == r)
    diagonal = own_slot.astype(jnp.int32)

    loads = [
        pltpu.make_async_copy(source, target, load_sem.at[index])
        for index, (source, target) in enumerate(
            (
                (align_hbm, align_ref),
                (mask_hbm, mask_ref),
                (wf_hbm, wf_ref),
                (wo_hbm, wo_ref),
                (wa_hbm, wa_ref),
                (chain_hbm, chain_ref),
                (table_hbm, table_ref),
                (pair_hbm, pair_ref),
                (wb_hbm, wb_ref),
                (wout_hbm, wout_ref),
            )
        )
    ]
    for load in loads:
        load.start()

    barrier = pltpu.get_barrier_semaphore()
    seq_peers = [lax.rem(q + d, n_seq) for d in range(n_seq)]
    res_peers = [lax.rem(r + d, n_res) for d in range(n_res)]
    for d in range(1, n_seq):
        pl.semaphore_signal(
            barrier, inc=1, device_id={"seq": seq_peers[d], "res": r}, device_id_type=MESH
        )
    for d in range(1, n_res):
        pl.semaphore_signal(
            barrier, inc=1, device_id={"seq": q, "res": res_peers[d]}, device_id_type=MESH
        )
    shares = n_seq // n_res
    for u in range(shares):

        def greet(u=u):
            pl.semaphore_signal(
                barrier,
                inc=1,
                device_id={"seq": u * n_res + r, "res": owner},
                device_id_type=MESH,
            )

        pl.when(jnp.logical_or(owner != r, u * n_res + r != q))(greet)

    for load in loads[:3]:
        load.wait()
    normed = layer_norm(align_ref[...])
    x_scr[...] = normed
    half = rows // 2
    x_buf[r] = jnp.concatenate([normed[:half], normed[half:]], axis=1).astype(BF16)
    mask_turned = mask_ref[...].astype(F32)
    eye = (iota((rd, rd), 0) == iota((rd, rd), 1)).astype(BF16)
    mask = dot(mask_turned.astype(BF16), eye, ((0,), (0,)))
    mask_wide = jnp.concatenate([mask_turned, jnp.zeros((rd, LANES - sd), F32)], axis=1)
    mask_buf[r] = mask_wide
    wf = wf_ref[...]
    wf_wide = jnp.concatenate([wf, wf], axis=1)
    per = LANES // co
    lane_block = iota((sd, LANES), 1) // co
    for g in range(rd // per):
        left = jnp.zeros((sd, LANES), F32)
        right = jnp.zeros((sd, LANES), F32)
        for m in range(per):
            i = g * per + m
            factor = dot(x_scr[pl.ds(i, sd, stride=rd), :].astype(BF16), wf_wide)
            factor = factor * mask[:, i : i + 1]
            left_at = (co * m) % LANES
            right_at = (co * m - co) % LANES
            left = jnp.where(lane_block == m, pltpu.roll(factor, left_at, 1) if left_at else factor, left)
            right = jnp.where(
                lane_block == m, pltpu.roll(factor, right_at, 1) if right_at else factor, right
            )
        left_buf[q, :, g * LANES : (g + 1) * LANES] = left.astype(BF16)
        right_own[:, g * LANES : (g + 1) * LANES] = right.astype(BF16)
    mask_pad = jnp.concatenate([mask, jnp.zeros((sd, LANES - rd), F32)], axis=1).astype(BF16)
    left_buf[q, :, fl : fl + LANES] = mask_pad
    right_own[:, fl : fl + LANES] = mask_pad

    pl.semaphore_wait(barrier, (n_seq - 1) + (n_res - 1) + ratio - diagonal)

    def right_copy(t):
        return pltpu.make_async_remote_copy(
            src_ref=right_own,
            dst_ref=right_buf.at[q],
            send_sem=send_r.at[t],
            recv_sem=recv_r.at[q],
            device_id={"seq": r * ratio + t, "res": relay},
            device_id_type=MESH,
        )

    def forward_copy(u, d):
        slot = u * n_res + r
        return pltpu.make_async_remote_copy(
            src_ref=right_buf.at[slot],
            dst_ref=right_buf.at[slot],
            send_sem=send_f.at[u * n_res + d],
            recv_sem=recv_r.at[slot],
            device_id={"seq": q, "res": res_peers[d]},
            device_id_type=MESH,
        )

    def right_arrival(slot):
        pltpu.make_async_remote_copy(
            src_ref=right_own,
            dst_ref=right_buf.at[slot],
            send_sem=send_r.at[0],
            recv_sem=recv_r.at[slot],
            device_id={"seq": q, "res": res_peers[1]},
            device_id_type=MESH,
        ).wait_recv()

    def left_copy(d):
        return pltpu.make_async_remote_copy(
            src_ref=left_buf.at[q],
            dst_ref=left_buf.at[q],
            send_sem=send_l.at[d],
            recv_sem=recv_l.at[d],
            device_id={"seq": seq_peers[d], "res": r},
            device_id_type=MESH,
        )

    def x_copy(d):
        return pltpu.make_async_remote_copy(
            src_ref=x_buf.at[r],
            dst_ref=x_buf.at[r],
            send_sem=send_x.at[d],
            recv_sem=recv_x.at[d],
            device_id={"seq": q, "res": res_peers[d]},
            device_id_type=MESH,
        )

    def mask_copy(d):
        return pltpu.make_async_remote_copy(
            src_ref=mask_buf.at[r],
            dst_ref=mask_buf.at[r],
            send_sem=send_m.at[d],
            recv_sem=recv_m.at[d],
            device_id={"seq": q, "res": res_peers[d]},
            device_id_type=MESH,
        )

    def each_right(action):
        for t in range(ratio):
            pl.when(jnp.logical_or(relay != r, r * ratio + t != q))(functools.partial(action, t))

    each_right(lambda t: right_copy(t).start())
    for d in range(1, n_seq):
        left_copy(d).start()

    @pl.when(own_slot)
    def _():
        right_buf[q] = right_own[...]

    for load in loads[3:]:
        load.wait()
    wo_high, wo_low = split(wo_ref[...])
    wsplit[:, :cz] = wo_high
    wsplit[:, cz:] = wo_low
    wa_diag[...] = jnp.zeros_like(wa_diag)
    wa_diag[:ch, : 4 * inner] = wa_ref[...]
    wa_diag[ch:, 4 * inner :] = wa_ref[...]

    for u in range(shares):
        slot = u * n_res + r
        pl.when(jnp.logical_or(owner != r, slot != q))(functools.partial(right_arrival, slot))
        for d in range(1, n_res):
            forward_copy(u, d).start()
    for d in range(1, n_res):
        x_copy(d).start()
        mask_copy(d).start()

    row = iota((rd, LANES), 0)
    lane = iota((rd, LANES), 1)
    reach = (bins - 2) // 2
    row_chain = jnp.zeros((rd, LANES), jnp.int32)
    for i in range(rd):
        row_chain = jnp.where(row == i, chain_ref[r * rd + i], row_chain)
    tab_high, tab_low = split(
        jnp.concatenate([table_ref[...], jnp.zeros((LANES - bins, cz), F32)], axis=0)
    )
    hot = []
    for j in range(cb):
        column = q * cb + j
        bin_ = jnp.where(
            row_chain == chain_ref[column],
            jnp.clip(row + r * rd - column + reach, 0, 2 * reach),
            2 * reach + 1,
        )
        hot.append(jnp.where(lane == bin_, 1.0, 0.0).astype(BF16))
    hot = jnp.concatenate(hot, axis=0)
    relative = dot(hot, tab_high) + dot(hot, tab_low)
    for j in range(cb):
        base_scr[j * rd : (j + 1) * rd] = (
            pair_ref[pl.ds(j, rd, stride=cb), :] + relative[j * rd : (j + 1) * rd]
        )

    spread = (iota((heads, LANES), 1) // rd == iota((heads, LANES), 0)).astype(F32)
    wb_high, wb_low = split(dot(wb_ref[...], spread, ((0,), (0,)), PRECISE))
    wb_both = jnp.concatenate([wb_high, wb_low], axis=1)

    def project(block):
        features = dot(x_buf[block], wa_diag[...])
        for part in range(2):
            at = 4 * inner * part
            qk_scr[block, part * half : (part + 1) * half] = features[:, at : at + LANES].astype(BF16)
            vg_scr[block, part * half : (part + 1) * half] = features[
                :, at + LANES : at + 2 * LANES
            ].astype(BF16)
        return features

    own = project(r)
    for part in range(2):
        at = 4 * inner * part
        place = slice(part * half, (part + 1) * half)
        q_scr[place] = pltpu.roll(own[:, at : at + LANES], inner, 1).astype(BF16)
        gate_scr[place] = jax.nn.sigmoid(
            pltpu.roll(own[:, at + LANES : at + 2 * LANES], inner, 1)
        )

    for d in range(1, n_seq):
        left_copy(d).wait_recv()
    for d in range(1, n_res):
        for u in range(shares):
            right_arrival(u * n_res + res_peers[d])

    left_all = left_buf[:, :, :fl].reshape(n_seq * sd, fl)
    block = iota((rd, LANES), 1) // co
    block_tall = jnp.concatenate([block] * (co // per), axis=0)
    for g in range(cb // per):
        at = g * LANES
        if ratio > 1:
            at = pl.multiple_of(lax.rem(q, ratio) * (cb * co) + g * LANES, LANES)
        right_part = right_buf[:, :, pl.ds(at, LANES)].reshape(n_seq * sd, LANES)
        outer_scr[g] = dot(left_all, right_part, ((0,), (0,)))
        tall = [
            jnp.concatenate(
                [outer_scr[g, pl.ds(per * k + m, rd, stride=co), :] for k in range(co // per)], axis=0
            )
            for m in range(per)
        ]
        for jj in range(per):
            total = None
            for m in range(per):
                shift = (co * (m - jj)) % LANES
                moved = pltpu.roll(tall[m], shift, 1) if shift else tall[m]
                total = moved if total is None else jnp.where(block_tall == m, moved, total)
            high, low = split(total)
            place = slice((g * per + jj) * rd, (g * per + jj + 1) * rd)
            for k in range(co // per):
                lhs_high[place, k * LANES : (k + 1) * LANES] = high[k * rd : (k + 1) * rd]
                lhs_low[place, k * LANES : (k + 1) * LANES] = low[k * rd : (k + 1) * rd]
    both = dot(lhs_high[...], wsplit[...])
    update = both[:, :cz] + both[:, cz:] + dot(lhs_low[...], wsplit[:, :cz])
    counted = dot(
        left_buf[:, :, fl : fl + LANES].reshape(n_seq * sd, LANES),
        right_buf[:, :, fl : fl + LANES].reshape(n_seq * sd, LANES),
        ((0,), (0,)),
    )[:rd]
    if ratio > 1:
        counted = pltpu.roll(counted, LANES - lax.rem(q, ratio) * cb, 1)
    scale = 1.0 / jnp.maximum(counted, 1.0)
    scale = jnp.concatenate(
        [jnp.broadcast_to(scale[:, j : j + 1], (rd, LANES)) for j in range(cb)], axis=0
    )
    pair_next = base_scr[...] + update * scale
    for j in range(cb):
        pair_out[pl.ds(j, rd, stride=cb), :] = pair_next[j * rd : (j + 1) * rd]
    n_high, n_low = split(layer_norm(pair_next))
    both = dot(n_high, wb_both)
    head = both[:, :LANES] + both[:, LANES:] + dot(n_low, wb_high)
    keep = iota((pairs, LANES), 0) % rd == iota((pairs, LANES), 1) % rd
    head = jnp.where(keep, head, 0.0).reshape(cb, rd, LANES)
    bias_own[:cb] = jnp.sum(head, axis=1)

    def bias_copy(d):
        return pltpu.make_async_remote_copy(
            src_ref=bias_own,
            dst_ref=bias_buf.at[q],
            send_sem=send_b.at[d],
            recv_sem=recv_b.at[d],
            device_id={"seq": seq_peers[d], "res": r},
            device_id_type=MESH,
        )

    for d in range(1, n_seq):
        bias_copy(d).start()
    bias_buf[q] = bias_own[...]

    for d in range(1, n_res):
        x_copy(d).wait_recv()
        mask_copy(d).wait_recv()
    for d in range(1, n_res):
        project(lax.rem(r + n_res - d, n_res))
    wide = heads * rd
    wide_row = iota((wide, LANES), 0) // rd
    wide_lane = iota((wide, LANES), 1)
    query_mask = jnp.where((wide_lane - inner) // hd == wide_row, 1.0, 0.0)
    query_mask = jnp.where(wide_lane >= inner, query_mask, 0.0).astype(BF16)
    out_mask = wide_lane // hd == wide_row
    score_scale = 1.0 / math.sqrt(hd)
    for s in range(sd):
        at = slice(s * rd, (s + 1) * rd)
        keys = qk_scr[:, at].reshape(residues, LANES)
        queries = jnp.concatenate([q_scr[at]] * heads, axis=0) * query_mask
        score_scr[s] = dot(keys, queries, ((1,), (1,))) * score_scale
    mask_bias = 1000000000.0 * (mask_buf[...].reshape(residues, LANES) - 1.0)

    for d in range(1, n_seq):
        bias_copy(d).wait_recv()
    for j in range(n_seq):
        bias_scr[j * cb : (j + 1) * cb] = bias_buf[j, :cb]
    bias = bias_scr[...]
    for s in range(sd):
        at = slice(s * rd, (s + 1) * rd)
        scores = score_scr[s] + bias + mask_bias[:, s : s + 1]
        weights = jnp.exp(scores - jnp.max(scores, 0, keepdims=True))
        weights = (weights * (1.0 / jnp.sum(weights, 0, keepdims=True))).astype(BF16)
        values = vg_scr[:, at].reshape(residues, LANES)
        mixed = jnp.where(out_mask, dot(weights, values, ((0,), (0,))), 0.0)
        att_scr[at] = jnp.sum(mixed.reshape(heads, rd, LANES), axis=0)
    gated = (gate_scr[...] * att_scr[...]).astype(BF16)[:, :inner]
    align_out[...] = align_ref[...] + dot(gated, wout_ref[...])

    each_right(lambda t: right_copy(t).wait_send())
    for u in range(shares):
        for d in range(1, n_res):
            forward_copy(u, d).wait_send()
    for d in range(1, n_seq):
        left_copy(d).wait_send()
        bias_copy(d).wait_send()
    for d in range(1, n_res):
        x_copy(d).wait_send()
        mask_copy(d).wait_send()


def solution(mesh):
    n_seq, n_res = mesh.shape["seq"], mesh.shape["res"]

    def body(align, mask, pair, chain, table, w_factors, w_outer, w_bias, w_attention, w_output):
        sd, rd, ch = align.shape
        cb, cz = pair.shape[1:]
        co = w_factors.shape[1] // 2
        heads = w_bias.shape[1]
        inner = w_attention.shape[1] // 4
        bins = table.shape[0]
        rows, pairs, residues = sd * rd, rd * cb, n_res * rd
        fl = rd * co
        per = LANES // co
        slot = max(cb, 8)
        sizes = (sd, rd, ch, cb, cz, co, heads, inner // heads, bins)
        vmem = pl.BlockSpec(memory_space=pltpu.VMEM)
        hbm = pl.BlockSpec(memory_space=pltpu.HBM)
        dma = pltpu.SemaphoreType.DMA
        pair_next, align_next = pl.pallas_call(
            functools.partial(kernel, n_seq, n_res, sizes),
            out_shape=(
                jax.ShapeDtypeStruct((pairs, cz), F32),
                jax.ShapeDtypeStruct((rows, ch), F32),
            ),
            in_specs=[hbm] * 10,
            out_specs=(vmem, vmem),
            scratch_shapes=[
                pltpu.VMEM((rows, ch), F32),
                pltpu.VMEM((rd, sd), jnp.int32),
                pltpu.VMEM((pairs, cz), F32),
                pltpu.SMEM((residues,), jnp.int32),
                pltpu.VMEM((bins, cz), F32),
                pltpu.VMEM((ch, 2 * co), BF16),
                pltpu.VMEM((co * co, cz), F32),
                pltpu.VMEM((heads, cz), F32),
                pltpu.VMEM((ch, 4 * inner), BF16),
                pltpu.VMEM((inner, ch), BF16),
                dma((10,)),
                pltpu.VMEM((rows, ch), F32),
                pltpu.VMEM((n_seq, sd, fl + LANES), BF16),
                pltpu.VMEM((n_seq, sd, fl + LANES), BF16),
                pltpu.VMEM((sd, fl + LANES), BF16),
                pltpu.VMEM((n_res, rows // 2, 2 * ch), BF16),
                pltpu.VMEM((n_res, rd, LANES), F32),
                pltpu.VMEM((n_seq, slot, LANES), F32),
                pltpu.VMEM((slot, LANES), F32),
                pltpu.VMEM((residues, LANES), F32),
                pltpu.VMEM((pairs, cz), F32),
                pltpu.VMEM((co * co, 2 * cz), BF16),
                pltpu.VMEM((2 * ch, 8 * inner), BF16),
                pltpu.VMEM((n_res, rows, LANES), BF16),
                pltpu.VMEM((n_res, rows, LANES), BF16),
                pltpu.VMEM((rows, LANES), BF16),
                pltpu.VMEM((rows, LANES), F32),
                pltpu.VMEM((cb // per, fl, LANES), F32),
                pltpu.VMEM((pairs, co * co), BF16),
                pltpu.VMEM((pairs, co * co), BF16),
                pltpu.VMEM((rows, LANES), F32),
                pltpu.VMEM((sd, residues, LANES), F32),
                dma((n_seq,)),
                dma((n_seq,)),
                dma((rd // cb,)),
                dma((n_seq,)),
                dma((n_seq,)),
                dma((n_res,)),
                dma((n_res,)),
                dma((n_res,)),
                dma((n_res,)),
                dma((n_seq,)),
                dma((n_seq,)),
            ],
            compiler_params=pltpu.CompilerParams(
                collective_id=0, has_side_effects=True, vmem_limit_bytes=64 * 1024 * 1024 - 65536
            ),
        )(
            align.reshape(rows, ch),
            mask.T,
            pair.reshape(pairs, cz),
            chain,
            table,
            w_factors,
            w_outer,
            w_bias.T,
            w_attention,
            w_output,
        )
        return pair_next.reshape(rd, cb, cz), align_next.reshape(sd, rd, ch)

    in_specs = (
        P(("groups", "seq"), "res", None),
        P(("groups", "seq"), "res"),
        P(("groups", "res"), "seq", None),
        P("groups"),
        P(),
        P(),
        P(),
        P(),
        P(),
        P(),
    )
    out_specs = (P(("groups", "res"), "seq", None), P(("groups", "seq"), "res", None))
    return jax.shard_map(body, mesh=mesh, in_specs=in_specs, out_specs=out_specs, check_vma=False)
```

```python
import functools
import math

import jax
import jax.numpy as jnp
from jax import lax
from jax.experimental import pallas as pl
from jax.experimental.pallas import tpu as pltpu
from jax.sharding import PartitionSpec as P

EPSILON = 1e-05
PRECISE = lax.Precision.HIGHEST
MESH = pl.DeviceIdType.MESH
F32 = jnp.float32
BF16 = jnp.bfloat16
LANES = 128


def iota(shape, dim):
    return lax.broadcasted_iota(jnp.int32, shape, dim)


def dot(a, b, dims=((1,), (0,)), precision=None):
    return lax.dot_general(
        a, b, (dims, ((), ())), precision=precision, preferred_element_type=F32
    )


def layer_norm(values):
    average = jnp.mean(values, -1, keepdims=True)
    centred = values - average
    variance = jnp.mean(centred * centred, -1, keepdims=True)
    return centred * lax.rsqrt(variance + EPSILON)


def split(values):
    high = values.astype(BF16)
    return high, (values - high.astype(F32)).astype(BF16)


def kernel(
    n_seq,
    n_res,
    sizes,
    align_hbm,
    mask_hbm,
    pair_hbm,
    chain_hbm,
    table_hbm,
    wf_hbm,
    wo_hbm,
    wb_hbm,
    wa_hbm,
    wout_hbm,
    pair_hbm_out,
    align_hbm_out,
    pair_out,
    align_out,
    store_sem,
    align_ref,
    mask_ref,
    pair_ref,
    chain_ref,
    table_ref,
    wf_ref,
    wo_ref,
    wb_ref,
    wa_ref,
    wout_ref,
    load_sem,
    x_scr,
    left_buf,
    right_buf,
    right_own,
    x_buf,
    mask_buf,
    bias_buf,
    bias_own,
    bias_scr,
    base_scr,
    wsplit,
    wa_diag,
    qk_scr,
    vg_scr,
    q_scr,
    gate_scr,
    outer_scr,
    lhs_high,
    lhs_low,
    att_scr,
    score_scr,
    send_l,
    recv_l,
    send_r,
    send_f,
    recv_r,
    send_x,
    recv_x,
    send_m,
    recv_m,
    send_b,
    recv_b,
):
    sd, rd, ch, cb, cz, co, heads, hd, bins = sizes
    inner = heads * hd
    ratio = rd // cb
    rows = sd * rd
    pairs = rd * cb
    residues = n_res * rd
    fl = rd * co
    q = lax.axis_index("seq")
    r = lax.axis_index("res")
    owner = q // ratio
    relay = lax.rem(q, n_res)
    own_slot = jnp.logical_and(owner == r, relay == r)
    diagonal = own_slot.astype(jnp.int32)

    loads = [
        pltpu.make_async_copy(source, target, load_sem.at[index])
        for index, (source, target) in enumerate(
            (
                (align_hbm, align_ref),
                (mask_hbm, mask_ref),
                (wf_hbm, wf_ref),
                (wo_hbm, wo_ref),
                (wa_hbm, wa_ref),
                (chain_hbm, chain_ref),
                (table_hbm, table_ref),
                (pair_hbm, pair_ref),
                (wb_hbm, wb_ref),
                (wout_hbm, wout_ref),
            )
        )
    ]
    for load in loads:
        load.start()

    barrier = pltpu.get_barrier_semaphore()
    seq_peers = [lax.rem(q + d, n_seq) for d in range(n_seq)]
    res_peers = [lax.rem(r + d, n_res) for d in range(n_res)]
    for d in range(1, n_seq):
        pl.semaphore_signal(
            barrier, inc=1, device_id={"seq": seq_peers[d], "res": r}, device_id_type=MESH
        )
    for d in range(1, n_res):
        pl.semaphore_signal(
            barrier, inc=1, device_id={"seq": q, "res": res_peers[d]}, device_id_type=MESH
        )
    shares = n_seq // n_res
    for u in range(shares):

        def greet(u=u):
            pl.semaphore_signal(
                barrier,
                inc=1,
                device_id={"seq": u * n_res + r, "res": owner},
                device_id_type=MESH,
            )

        pl.when(jnp.logical_or(owner != r, u * n_res + r != q))(greet)

    for load in loads[:3]:
        load.wait()
    normed = layer_norm(align_ref[...])
    x_scr[...] = normed
    half = rows // 2
    x_buf[r] = jnp.concatenate([normed[:half], normed[half:]], axis=1).astype(BF16)
    mask_turned = mask_ref[...].astype(F32)
    eye = (iota((rd, rd), 0) == iota((rd, rd), 1)).astype(BF16)
    mask = dot(mask_turned.astype(BF16), eye, ((0,), (0,)))
    mask_wide = jnp.concatenate([mask_turned, jnp.zeros((rd, LANES - sd), F32)], axis=1)
    mask_buf[r] = mask_wide
    wf = wf_ref[...]
    wf_wide = jnp.concatenate([wf, wf], axis=1)
    per = LANES // co
    lane_block = iota((sd, LANES), 1) // co
    for g in range(rd // per):
        left = jnp.zeros((sd, LANES), F32)
        right = jnp.zeros((sd, LANES), F32)
        for m in range(per):
            i = g * per + m
            factor = dot(x_scr[pl.ds(i, sd, stride=rd), :].astype(BF16), wf_wide)
            factor = factor * mask[:, i : i + 1]
            left_at = (co * m) % LANES
            right_at = (co * m - co) % LANES
            left = jnp.where(lane_block == m, pltpu.roll(factor, left_at, 1) if left_at else factor, left)
            right = jnp.where(
                lane_block == m, pltpu.roll(factor, right_at, 1) if right_at else factor, right
            )
        left_buf[q, :, g * LANES : (g + 1) * LANES] = left.astype(BF16)
        right_own[:, g * LANES : (g + 1) * LANES] = right.astype(BF16)
    mask_pad = jnp.concatenate([mask, jnp.zeros((sd, LANES - rd), F32)], axis=1).astype(BF16)
    left_buf[q, :, fl : fl + LANES] = mask_pad
    right_own[:, fl : fl + LANES] = mask_pad

    pl.semaphore_wait(barrier, (n_seq - 1) + (n_res - 1) + ratio - diagonal)

    def right_copy(t):
        return pltpu.make_async_remote_copy(
            src_ref=right_own,
            dst_ref=right_buf.at[q],
            send_sem=send_r.at[t],
            recv_sem=recv_r.at[q],
            device_id={"seq": r * ratio + t, "res": relay},
            device_id_type=MESH,
        )

    def forward_copy(u, d):
        slot = u * n_res + r
        return pltpu.make_async_remote_copy(
            src_ref=right_buf.at[slot],
            dst_ref=right_buf.at[slot],
            send_sem=send_f.at[u * n_res + d],
            recv_sem=recv_r.at[slot],
            device_id={"seq": q, "res": res_peers[d]},
            device_id_type=MESH,
        )

    def right_arrival(slot):
        pltpu.make_async_remote_copy(
            src_ref=right_own,
            dst_ref=right_buf.at[slot],
            send_sem=send_r.at[0],
            recv_sem=recv_r.at[slot],
            device_id={"seq": q, "res": res_peers[1]},
            device_id_type=MESH,
        ).wait_recv()

    def left_copy(d):
        return pltpu.make_async_remote_copy(
            src_ref=left_buf.at[q],
            dst_ref=left_buf.at[q],
            send_sem=send_l.at[d],
            recv_sem=recv_l.at[d],
            device_id={"seq": seq_peers[d], "res": r},
            device_id_type=MESH,
        )

    def x_copy(d):
        return pltpu.make_async_remote_copy(
            src_ref=x_buf.at[r],
            dst_ref=x_buf.at[r],
            send_sem=send_x.at[d],
            recv_sem=recv_x.at[d],
            device_id={"seq": q, "res": res_peers[d]},
            device_id_type=MESH,
        )

    def mask_copy(d):
        return pltpu.make_async_remote_copy(
            src_ref=mask_buf.at[r],
            dst_ref=mask_buf.at[r],
            send_sem=send_m.at[d],
            recv_sem=recv_m.at[d],
            device_id={"seq": q, "res": res_peers[d]},
            device_id_type=MESH,
        )

    def each_right(action):
        for t in range(ratio):
            pl.when(jnp.logical_or(relay != r, r * ratio + t != q))(functools.partial(action, t))

    each_right(lambda t: right_copy(t).start())
    for d in range(1, n_seq):
        left_copy(d).start()

    @pl.when(own_slot)
    def _():
        right_buf[q] = right_own[...]

    for load in loads[3:]:
        load.wait()
    wo_high, wo_low = split(wo_ref[...])
    wsplit[:, :cz] = wo_high
    wsplit[:, cz:] = wo_low
    wa_diag[...] = jnp.zeros_like(wa_diag)
    wa_diag[:ch, : 4 * inner] = wa_ref[...]
    wa_diag[ch:, 4 * inner :] = wa_ref[...]

    for u in range(shares):
        slot = u * n_res + r
        pl.when(jnp.logical_or(owner != r, slot != q))(functools.partial(right_arrival, slot))
        for d in range(1, n_res):
            forward_copy(u, d).start()
    for d in range(1, n_res):
        x_copy(d).start()
        mask_copy(d).start()

    row = iota((rd, LANES), 0)
    lane = iota((rd, LANES), 1)
    reach = (bins - 2) // 2
    row_chain = jnp.zeros((rd, LANES), jnp.int32)
    for i in range(rd):
        row_chain = jnp.where(row == i, chain_ref[r * rd + i], row_chain)
    tab_high, tab_low = split(
        jnp.concatenate([table_ref[...], jnp.zeros((LANES - bins, cz), F32)], axis=0)
    )
    hot = []
    for j in range(cb):
        column = q * cb + j
        bin_ = jnp.where(
            row_chain == chain_ref[column],
            jnp.clip(row + r * rd - column + reach, 0, 2 * reach),
            2 * reach + 1,
        )
        hot.append(jnp.where(lane == bin_, 1.0, 0.0).astype(BF16))
    hot = jnp.concatenate(hot, axis=0)
    relative = dot(hot, tab_high) + dot(hot, tab_low)
    for j in range(cb):
        base_scr[j * rd : (j + 1) * rd] = (
            pair_ref[pl.ds(j, rd, stride=cb), :] + relative[j * rd : (j + 1) * rd]
        )

    spread = (iota((heads, LANES), 1) // rd == iota((heads, LANES), 0)).astype(F32)
    wb_high, wb_low = split(dot(wb_ref[...], spread, ((0,), (0,)), PRECISE))
    wb_both = jnp.concatenate([wb_high, wb_low], axis=1)

    def project(block):
        features = dot(x_buf[block], wa_diag[...])
        for part in range(2):
            at = 4 * inner * part
            qk_scr[block, part * half : (part + 1) * half] = features[:, at : at + LANES].astype(BF16)
            vg_scr[block, part * half : (part + 1) * half] = features[
                :, at + LANES : at + 2 * LANES
            ].astype(BF16)
        return features

    own = project(r)
    for part in range(2):
        at = 4 * inner * part
        place = slice(part * half, (part + 1) * half)
        q_scr[place] = pltpu.roll(own[:, at : at + LANES], inner, 1).astype(BF16)
        gate_scr[place] = jax.nn.sigmoid(
            pltpu.roll(own[:, at + LANES : at + 2 * LANES], inner, 1)
        )

    for d in range(1, n_seq):
        left_copy(d).wait_recv()
    for d in range(1, n_res):
        for u in range(shares):
            right_arrival(u * n_res + res_peers[d])

    left_all = left_buf[:, :, :fl].reshape(n_seq * sd, fl)
    block = iota((rd, LANES), 1) // co
    block_tall = jnp.concatenate([block] * (co // per), axis=0)
    for g in range(cb // per):
        at = g * LANES
        if ratio > 1:
            at = pl.multiple_of(lax.rem(q, ratio) * (cb * co) + g * LANES, LANES)
        right_part = right_buf[:, :, pl.ds(at, LANES)].reshape(n_seq * sd, LANES)
        outer_scr[g] = dot(left_all, right_part, ((0,), (0,)))
        tall = [
            jnp.concatenate(
                [outer_scr[g, pl.ds(per * k + m, rd, stride=co), :] for k in range(co // per)], axis=0
            )
            for m in range(per)
        ]
        for jj in range(per):
            total = None
            for m in range(per):
                shift = (co * (m - jj)) % LANES
                moved = pltpu.roll(tall[m], shift, 1) if shift else tall[m]
                total = moved if total is None else jnp.where(block_tall == m, moved, total)
            high, low = split(total)
            place = slice((g * per + jj) * rd, (g * per + jj + 1) * rd)
            for k in range(co // per):
                lhs_high[place, k * LANES : (k + 1) * LANES] = high[k * rd : (k + 1) * rd]
                lhs_low[place, k * LANES : (k + 1) * LANES] = low[k * rd : (k + 1) * rd]
    both = dot(lhs_high[...], wsplit[...])
    update = both[:, :cz] + both[:, cz:] + dot(lhs_low[...], wsplit[:, :cz])
    counted = dot(
        left_buf[:, :, fl : fl + LANES].reshape(n_seq * sd, LANES),
        right_buf[:, :, fl : fl + LANES].reshape(n_seq * sd, LANES),
        ((0,), (0,)),
    )[:rd]
    if ratio > 1:
        counted = pltpu.roll(counted, LANES - lax.rem(q, ratio) * cb, 1)
    scale = 1.0 / jnp.maximum(counted, 1.0)
    scale = jnp.concatenate(
        [jnp.broadcast_to(scale[:, j : j + 1], (rd, LANES)) for j in range(cb)], axis=0
    )
    pair_next = base_scr[...] + update * scale
    for j in range(cb):
        pair_out[pl.ds(j, rd, stride=cb), :] = pair_next[j * rd : (j + 1) * rd]
    pair_store = pltpu.make_async_copy(pair_out, pair_hbm_out, store_sem.at[0])
    pair_store.start()
    n_high, n_low = split(layer_norm(pair_next))
    both = dot(n_high, wb_both)
    head = both[:, :LANES] + both[:, LANES:] + dot(n_low, wb_high)
    keep = iota((pairs, LANES), 0) % rd == iota((pairs, LANES), 1) % rd
    head = jnp.where(keep, head, 0.0).reshape(cb, rd, LANES)
    bias_own[:cb] = jnp.sum(head, axis=1)

    def bias_copy(d):
        return pltpu.make_async_remote_copy(
            src_ref=bias_own,
            dst_ref=bias_buf.at[q],
            send_sem=send_b.at[d],
            recv_sem=recv_b.at[d],
            device_id={"seq": seq_peers[d], "res": r},
            device_id_type=MESH,
        )

    for d in range(1, n_seq):
        bias_copy(d).start()
    bias_buf[q] = bias_own[...]

    for d in range(1, n_res):
        x_copy(d).wait_recv()
        mask_copy(d).wait_recv()
    for d in range(1, n_res):
        project(lax.rem(r + n_res - d, n_res))
    wide = heads * rd
    wide_row = iota((wide, LANES), 0) // rd
    wide_lane = iota((wide, LANES), 1)
    query_mask = jnp.where((wide_lane - inner) // hd == wide_row, 1.0, 0.0)
    query_mask = jnp.where(wide_lane >= inner, query_mask, 0.0).astype(BF16)
    out_mask = wide_lane // hd == wide_row
    score_scale = 1.0 / math.sqrt(hd)
    for s in range(sd):
        at = slice(s * rd, (s + 1) * rd)
        keys = qk_scr[:, at].reshape(residues, LANES)
        queries = jnp.concatenate([q_scr[at]] * heads, axis=0) * query_mask
        score_scr[s] = dot(keys, queries, ((1,), (1,))) * score_scale
    mask_bias = 1000000000.0 * (mask_buf[...].reshape(residues, LANES) - 1.0)

    for d in range(1, n_seq):
        bias_copy(d).wait_recv()
    for j in range(n_seq):
        bias_scr[j * cb : (j + 1) * cb] = bias_buf[j, :cb]
    bias = bias_scr[...]
    for s in range(sd):
        at = slice(s * rd, (s + 1) * rd)
        scores = score_scr[s] + bias + mask_bias[:, s : s + 1]
        weights = jnp.exp(scores - jnp.max(scores, 0, keepdims=True))
        weights = (weights * (1.0 / jnp.sum(weights, 0, keepdims=True))).astype(BF16)
        values = vg_scr[:, at].reshape(residues, LANES)
        mixed = jnp.where(out_mask, dot(weights, values, ((0,), (0,))), 0.0)
        att_scr[at] = jnp.sum(mixed.reshape(heads, rd, LANES), axis=0)
    gated = (gate_scr[...] * att_scr[...]).astype(BF16)[:, :inner]
    align_out[...] = align_ref[...] + dot(gated, wout_ref[...])
    align_store = pltpu.make_async_copy(align_out, align_hbm_out, store_sem.at[1])
    align_store.start()
    pair_store.wait()

    each_right(lambda t: right_copy(t).wait_send())
    for u in range(shares):
        for d in range(1, n_res):
            forward_copy(u, d).wait_send()
    for d in range(1, n_seq):
        left_copy(d).wait_send()
        bias_copy(d).wait_send()
    for d in range(1, n_res):
        x_copy(d).wait_send()
        mask_copy(d).wait_send()
    align_store.wait()


def solution(mesh):
    n_seq, n_res = mesh.shape["seq"], mesh.shape["res"]

    def body(align, mask, pair, chain, table, w_factors, w_outer, w_bias, w_attention, w_output):
        sd, rd, ch = align.shape
        cb, cz = pair.shape[1:]
        co = w_factors.shape[1] // 2
        heads = w_bias.shape[1]
        inner = w_attention.shape[1] // 4
        bins = table.shape[0]
        rows, pairs, residues = sd * rd, rd * cb, n_res * rd
        fl = rd * co
        per = LANES // co
        slot = max(cb, 8)
        sizes = (sd, rd, ch, cb, cz, co, heads, inner // heads, bins)
        hbm = pl.BlockSpec(memory_space=pltpu.HBM)
        dma = pltpu.SemaphoreType.DMA
        pair_next, align_next = pl.pallas_call(
            functools.partial(kernel, n_seq, n_res, sizes),
            out_shape=(
                jax.ShapeDtypeStruct((pairs, cz), F32),
                jax.ShapeDtypeStruct((rows, ch), F32),
            ),
            in_specs=[hbm] * 10,
            out_specs=(hbm, hbm),
            scratch_shapes=[
                pltpu.VMEM((pairs, cz), F32),
                pltpu.VMEM((rows, ch), F32),
                dma((2,)),
                pltpu.VMEM((rows, ch), F32),
                pltpu.VMEM((rd, sd), jnp.int32),
                pltpu.VMEM((pairs, cz), F32),
                pltpu.SMEM((residues,), jnp.int32),
                pltpu.VMEM((bins, cz), F32),
                pltpu.VMEM((ch, 2 * co), BF16),
                pltpu.VMEM((co * co, cz), F32),
                pltpu.VMEM((heads, cz), F32),
                pltpu.VMEM((ch, 4 * inner), BF16),
                pltpu.VMEM((inner, ch), BF16),
                dma((10,)),
                pltpu.VMEM((rows, ch), F32),
                pltpu.VMEM((n_seq, sd, fl + LANES), BF16),
                pltpu.VMEM((n_seq, sd, fl + LANES), BF16),
                pltpu.VMEM((sd, fl + LANES), BF16),
                pltpu.VMEM((n_res, rows // 2, 2 * ch), BF16),
                pltpu.VMEM((n_res, rd, LANES), F32),
                pltpu.VMEM((n_seq, slot, LANES), F32),
                pltpu.VMEM((slot, LANES), F32),
                pltpu.VMEM((residues, LANES), F32),
                pltpu.VMEM((pairs, cz), F32),
                pltpu.VMEM((co * co, 2 * cz), BF16),
                pltpu.VMEM((2 * ch, 8 * inner), BF16),
                pltpu.VMEM((n_res, rows, LANES), BF16),
                pltpu.VMEM((n_res, rows, LANES), BF16),
                pltpu.VMEM((rows, LANES), BF16),
                pltpu.VMEM((rows, LANES), F32),
                pltpu.VMEM((cb // per, fl, LANES), F32),
                pltpu.VMEM((pairs, co * co), BF16),
                pltpu.VMEM((pairs, co * co), BF16),
                pltpu.VMEM((rows, LANES), F32),
                pltpu.VMEM((sd, residues, LANES), F32),
                dma((n_seq,)),
                dma((n_seq,)),
                dma((rd // cb,)),
                dma((n_seq,)),
                dma((n_seq,)),
                dma((n_res,)),
                dma((n_res,)),
                dma((n_res,)),
                dma((n_res,)),
                dma((n_seq,)),
                dma((n_seq,)),
            ],
            compiler_params=pltpu.CompilerParams(
                collective_id=0, has_side_effects=True, vmem_limit_bytes=64 * 1024 * 1024 - 65536
            ),
        )(
            align.reshape(rows, ch),
            mask.T,
            pair.reshape(pairs, cz),
            chain,
            table,
            w_factors,
            w_outer,
            w_bias.T,
            w_attention,
            w_output,
        )
        return pair_next.reshape(rd, cb, cz), align_next.reshape(sd, rd, ch)

    in_specs = (
        P(("groups", "seq"), "res", None),
        P(("groups", "seq"), "res"),
        P(("groups", "res"), "seq", None),
        P("groups"),
        P(),
        P(),
        P(),
        P(),
        P(),
        P(),
    )
    out_specs = (P(("groups", "res"), "seq", None), P(("groups", "seq"), "res", None))
    return jax.shard_map(body, mesh=mesh, in_specs=in_specs, out_specs=out_specs, check_vma=False)
```
